256 devices in a mesh: grp: 64 (over z_lo, x, y), sp: 4 (over z_hi, core).
Axes of the slice: x: 4, y: 4, z: 8 (z_hi: 2, z_lo: 4; z = z_hi * 4 + z_lo), core: 2. Of those that a mesh axis runs over, the one named last changes fastest.
Arguments:
- queries: bfloat16 [32768, 2048], P(('grp', 'sp')), may hold values from -6 to 6
- keys: bfloat16 [32768, 1024], P(('grp', 'sp')), may hold values from -6 to 6
- values: bfloat16 [32768, 1024], P(('grp', 'sp')), may hold values from -6 to 6
- doc_ids: int32 [32768], P(('grp', 'sp')), may hold values from 0 to 127, as said below
- w_out: bfloat16 [2048, 4608], P('sp', 'grp'), may hold values from -0.125 to 0.125
- cotangent: bfloat16 [32768, 4608], P(('grp', 'sp')), may hold values from -24 to 24
Outputs:
- mixed: bfloat16 [32768, 4608], P(('grp', 'sp'))
- query_grad: bfloat16 [32768, 2048], P(('grp', 'sp'))
- key_grad: bfloat16 [32768, 1024], P(('grp', 'sp'))
- value_grad: bfloat16 [32768, 1024], P(('grp', 'sp'))
- w_grad: float32 [2048, 4608], P('sp', 'grp')
The draws below stay inside these ranges and needn't reach their ends.
Inputs may be any that keep to these rules, and one draw needn't show every extreme that they name: `doc_ids`: each group of 512 consecutive tokens holds one or two whole documents; document numbers never fall along the tokens; every document holds 128 to 512 tokens, and some document holds exactly 512.
All inputs are finite; a program needn't handle non-finite values.
Results may differ from the reference program's by a relative error of at most 0.017.
Values may be sent and summed in bfloat16 or wider, within the bound.
No kernel may reach another device: no remote copies, remote signals or barrier semaphores. Data moves between devices by JAX's collectives and lax.ppermute only.
A program may use at most 128 MiB of HBM per device.

```python
import jax
import jax.numpy as jnp
from jax import lax

D = 4608
H = 16
KV = 8
HD = 128
TOK_DEV = 128
GROUP_TOK = 512
TOKENS = 32768
N_GRP = 64
N_SP = 4


def draw_doc_ids(key, part):
    key = jax.random.fold_in(key, 7)
    groups = TOKENS // GROUP_TOK
    cut_key, whole_key = jax.random.split(key)
    quarter = GROUP_TOK // 4
    cuts = jax.random.randint(cut_key, (groups,), quarter, GROUP_TOK - quarter + 1, dtype=jnp.int32)
    whole = jax.random.randint(whole_key, (), 0, groups - 1, dtype=jnp.int32)
    group_index = jnp.arange(groups, dtype=jnp.int32)
    cuts = jnp.where(group_index == whole, jnp.int32(GROUP_TOK), cuts)
    position = jnp.arange(GROUP_TOK, dtype=jnp.int32)
    second = (position[None, :] >= cuts[:, None]).astype(jnp.int32)
    ids = 2 * group_index[:, None] + second
    return ids.reshape(-1).astype(jnp.int32)


def raised(values, own_key, source, target, shards_of, factor):
    owner, partner = [(jnp.arange(values.shape[axis_at]) // (values.shape[axis_at] // shards_of)).reshape([-1 if axis == axis_at else 1 for axis in range(values.ndim)]) for axis_at in (source, target)]
    chosen = jax.random.permutation(own_key, shards_of)[partner]
    strong = (owner == chosen) | (owner == (partner + shards_of // 2) % shards_of)
    return jnp.where(strong, factor * values, values)


def block_levels(stream_key, extent, shards, smallest, top_value):
    gain = 1.0
    for dim, parts in shards:
        heights = jax.random.uniform(jax.random.fold_in(jax.random.fold_in(stream_key, 6), dim), (parts,), jnp.float32, smallest / len(shards), top_value / len(shards))
        gain = gain * jnp.repeat(jnp.exp(heights), extent[dim] // parts).reshape((-1,) + (1,) * (len(extent) - 1 - dim))
    return gain


def normal_values(own_key, dims, spread, limit, cuts=(), kind=jnp.bfloat16):
    result = jax.random.normal(own_key, dims, jnp.float32) * spread
    if len(cuts) > 0:
        result = block_levels(own_key, dims, cuts, -0.22, 0.18) * result
    return jnp.clip(result, min=-limit, max=limit).astype(kind)


def heavy_noise(rng, dims, scale, limit, shards, heavy, kind=jnp.bfloat16):
    drawn = scale * jax.random.normal(rng, dims, jnp.float32)
    if shards:
        drawn = drawn * block_levels(rng, dims, shards, -0.22, 0.18)
    return jnp.clip(raised(drawn, jax.random.fold_in(rng, 3), *heavy), -limit, limit).astype(kind)


def setup_inputs(seed: int = 0) -> dict:
    streams_of = jax.random.split(jax.random.key(seed), 7)
    return {
        "queries": normal_values(streams_of[0], (TOKENS, H * HD), 1.0, 6.0, ((0, 256),)),
        "keys": normal_values(streams_of[1], (TOKENS, KV * HD), 1.0, 6.0, ((0, 256),)),
        "values": normal_values(streams_of[2], (TOKENS, KV * HD), 1.0, 6.0, ((0, 256),)),
        "doc_ids": draw_doc_ids(jax.random.fold_in(streams_of[6], 71), 0),
        "w_out": normal_values(streams_of[4], (H * HD, D), (H * HD) ** -0.5, 0.125, ((0, 4), (1, 64))),
        "cotangent": heavy_noise(streams_of[5], (TOKENS, D), 1.0, 24.0, ((0, 256),), (0, 1, 256, 6.0)),
    }


query_scale = 1.0 / 12.0
softcap = 50.0


def attend_group(inputs):
    query_in, key_in, value_in, group_ids, grad_in = inputs
    length = query_in.shape[0]
    repeat = H // KV
    queries4 = query_in.astype(jnp.float32).reshape(length, KV, repeat, HD)
    keys3 = key_in.astype(jnp.float32).reshape(length, KV, HD)
    values3 = value_in.astype(jnp.float32).reshape(length, KV, HD)
    grads4 = grad_in.astype(jnp.float32).reshape(length, KV, repeat, HD)
    raw_scores = jnp.einsum("qgrd,kgd->grqk", queries4, keys3) * query_scale
    capped = softcap * jnp.tanh(raw_scores / softcap)
    position = jnp.arange(length, dtype=jnp.int32)
    visible = (group_ids[:, None] == group_ids[None, :]) & (position[:, None] >= position[None, :])
    weights = jnp.where(visible, jnp.exp(capped), jnp.float32(0.0))
    output_totals = jnp.sum(weights, axis=-1, keepdims=True)
    probability = weights / output_totals
    rounded = lax.optimization_barrier(probability.astype(jnp.bfloat16)).astype(jnp.float32)
    attended = jnp.einsum("grqk,kgd->qgrd", rounded, values3).astype(jnp.bfloat16)
    attended_wide = lax.optimization_barrier(attended).astype(jnp.float32)
    row_dots = jnp.einsum("qgrd,qgrd->grq", grads4, attended_wide)
    prob_grad = jnp.einsum("qgrd,kgd->grqk", grads4, values3)
    score_grad = probability * (prob_grad - row_dots[..., None]) * (1.0 - (capped / softcap) ** 2)
    score_grad = lax.optimization_barrier(score_grad.astype(jnp.bfloat16)).astype(jnp.float32)
    query_grad = (query_scale * jnp.einsum("grqk,kgd->qgrd", score_grad, keys3)).astype(jnp.bfloat16)
    key_grad = (query_scale * jnp.einsum("grqk,qgrd->kgd", score_grad, queries4)).astype(jnp.bfloat16)
    value_grad = jnp.einsum("grqk,qgrd->kgd", rounded, grads4).astype(jnp.bfloat16)
    return (attended.reshape(length, H * HD), query_grad.reshape(length, H * HD),
            key_grad.reshape(length, KV * HD), value_grad.reshape(length, KV * HD))


def reference(queries, keys, values, doc_ids, w_out, cotangent):
    grads_out = jnp.dot(cotangent, w_out.T, preferred_element_type=jnp.float32).astype(jnp.bfloat16)
    group_len = N_SP * TOK_DEV

    def split(array):
        return array.reshape((N_GRP, group_len) + array.shape[1:])

    attended, query_grad, key_grad, value_grad = lax.map(
        attend_group, (split(queries), split(keys), split(values), split(doc_ids), split(grads_out)))
    attended = attended.reshape(N_GRP * group_len, H * HD)
    mixed = jnp.dot(attended, w_out, preferred_element_type=jnp.float32).astype(jnp.bfloat16)
    w_grad = jnp.dot(attended.T, cotangent, preferred_element_type=jnp.float32)
    return (mixed, query_grad.reshape(-1, H * HD), key_grad.reshape(-1, KV * HD),
            value_grad.reshape(-1, KV * HD), w_grad)
```

```python
import jax
import jax.numpy as jnp
from jax import lax
from jax.experimental import pallas as pl
from jax.experimental.pallas import tpu as pltpu
from jax.sharding import Mesh, PartitionSpec as P

HD = 128
SCALE = 1.0 / 12.0
CAP = 50.0
F32 = jnp.float32
BF16 = jnp.bfloat16
NT = (((1,), (1,)), ((), ()))
TN = (((0,), (0,)), ((), ()))
Z = ("zl", "zh")


def dot(a, b, dims=(((1,), (0,)), ((), ()))):
    return lax.dot_general(a, b, dims, preferred_element_type=F32)


def shift(a, axis, step):
    return lax.ppermute(a, axis, [(i, (i + step) % 4) for i in range(4)])


def z_index(z):
    z = z % 8
    return (z % 4) * 2 + z // 4


def shift_z(a, step):
    return lax.ppermute(a, Z, [(z_index(z), z_index(z + step)) for z in range(8)])


def swap_core(a):
    return lax.ppermute(a, "c", [(0, 1), (1, 0)])


def pick(a, index, axis):
    return lax.dynamic_index_in_dim(a, index, axis, keepdims=False)


def forward_kernel(q_ref, ko_ref, kx_ref, vo_ref, vx_ref, m_ref, att_ref, p_ref, d_ref):
    for r in range(2):
        cols = slice(r * HD, (r + 1) * HD)
        q = q_ref[:, cols]
        parts = []
        for half, k_ref in ((0, ko_ref), (1, kx_ref)):
            t = jnp.tanh(dot(q, k_ref[...], NT) * (SCALE / CAP))
            w = jnp.exp(CAP * t) * m_ref[:, half * 256 : half * 256 + 256]
            parts.append((t, w))
        total = sum(jnp.sum(w, axis=-1, keepdims=True) for _, w in parts)
        inverse = 1.0 / total
        att = 0.0
        for half, v_ref in ((0, vo_ref), (1, vx_ref)):
            t, w = parts[half]
            p = w * inverse
            rounded = p.astype(BF16)
            keys = slice(half * 256, half * 256 + 256)
            p_ref[r, :, keys] = rounded
            d_ref[r, :, keys] = p * (1.0 - t * t)
            att = att + dot(rounded, v_ref[...])
        att_ref[:, cols] = att.astype(BF16)


def backward_kernel(
    q_ref, ko_ref, kx_ref, vo_ref, vx_ref, att_ref, p_ref, d_ref, g_ref,
    dq_ref, dko_ref, dkx_ref, dvo_ref, dvx_ref,
):
    dk = [0.0, 0.0]
    dv = [0.0, 0.0]
    for r in range(2):
        cols = slice(r * HD, (r + 1) * HD)
        q = q_ref[:, cols]
        g = g_ref[:, cols]
        row = jnp.sum(g.astype(F32) * att_ref[:, cols].astype(F32), axis=-1, keepdims=True)
        dq = 0.0
        for half, k_ref, v_ref in ((0, ko_ref, vo_ref), (1, kx_ref, vx_ref)):
            keys = slice(half * 256, half * 256 + 256)
            dp = dot(g, v_ref[...], NT)
            ds = (d_ref[r, :, keys] * (dp - row)).astype(BF16)
            dq = dq + dot(ds, k_ref[...])
            dk[half] = dk[half] + dot(ds, q, TN)
            dv[half] = dv[half] + dot(p_ref[r, :, keys], g, TN)
        dq_ref[:, cols] = (dq * SCALE).astype(BF16)
    dko_ref[...] = dk[0] * SCALE
    dkx_ref[...] = (dk[1] * SCALE).astype(BF16)
    dvo_ref[...] = dv[0]
    dvx_ref[...] = dv[1].astype(BF16)


def pair_spec():
    return pl.BlockSpec((256, 2 * HD), lambda g: (0, g))


def key_spec():
    return pl.BlockSpec((256, HD), lambda g: (0, g))


def score_spec():
    return pl.BlockSpec((2, 256, 512), lambda g: (g, 0, 0))


def attend(q, ko, kx, vo, vx, mask):
    return pl.pallas_call(
        forward_kernel,
        grid=(4,),
        in_specs=[pair_spec(), key_spec(), key_spec(), key_spec(), key_spec(),
                  pl.BlockSpec((256, 512), lambda g: (0, 0))],
        out_specs=[pair_spec(), score_spec(), score_spec()],
        out_shape=[
            jax.ShapeDtypeStruct((256, 1024), BF16),
            jax.ShapeDtypeStruct((8, 256, 512), BF16),
            jax.ShapeDtypeStruct((8, 256, 512), F32),
        ],
        cost_estimate=pl.CostEstimate(
            flops=8 * 256 * 512 * 128 * 4, bytes_accessed=9 << 20, transcendentals=8 * 256 * 512 * 2
        ),
        compiler_params=pltpu.CompilerParams(vmem_limit_bytes=32 << 20),
        name="attend",
    )(q, ko, kx, vo, vx, mask)


def attend_back(q, ko, kx, vo, vx, att, p, d, g):
    return pl.pallas_call(
        backward_kernel,
        grid=(4,),
        in_specs=[pair_spec(), key_spec(), key_spec(), key_spec(), key_spec(),
                  pair_spec(), score_spec(), score_spec(), pair_spec()],
        out_specs=[pair_spec(), key_spec(), key_spec(), key_spec(), key_spec()],
        out_shape=[
            jax.ShapeDtypeStruct((256, 1024), BF16),
            jax.ShapeDtypeStruct((256, 512), F32),
            jax.ShapeDtypeStruct((256, 512), BF16),
            jax.ShapeDtypeStruct((256, 512), F32),
            jax.ShapeDtypeStruct((256, 512), BF16),
        ],
        cost_estimate=pl.CostEstimate(
            flops=8 * 256 * 512 * 128 * 8, bytes_accessed=11 << 20, transcendentals=0
        ),
        compiler_params=pltpu.CompilerParams(vmem_limit_bytes=32 << 20),
        name="attend_back",
    )(q, ko, kx, vo, vx, att, p, d, g)


def place(buffer, block, index, axis):
    return lax.dynamic_update_index_in_dim(buffer, block, index, axis)


def gather_axis(block, axis, at):
    me = lax.axis_index(axis)
    shape = block.shape[:at] + (4,) + block.shape[at:]
    out = place(jnp.zeros(shape, block.dtype), block, me, at)
    for step in (1, 3, 2):
        out = place(out, shift(block, axis, step), (me - step) % 4, at)
    return out


def gather_z(block):
    z = lax.axis_index("zh") * 4 + lax.axis_index("zl")

    def put(out, part, at):
        at = at % 8
        return lax.dynamic_update_slice(out, part[None, None], (at // 4, at % 4, 0, 0))

    out = put(jnp.zeros((2, 4) + block.shape, block.dtype), block, z)
    for step in (1, 7, 2, 6, 3, 5, 4):
        out = put(out, shift_z(block, step), z - step)
    return out


def scatter_axis(blocks, axis, at):
    me = lax.axis_index(axis)
    total = pick(blocks, me, at).astype(F32)
    for step in (1, 3, 2):
        total = total + shift(pick(blocks, (me + step) % 4, at), axis, step).astype(F32)
    return total.astype(BF16)


def scatter_z(first, second):
    blocks = jnp.stack([first, second])
    z = lax.axis_index("zh") * 4 + lax.axis_index("zl")

    def take(at):
        at = at % 8
        part = lax.dynamic_slice(blocks, (at // 4, at % 4, 0, 0), (1, 1) + blocks.shape[2:])
        return part.reshape(blocks.shape[2:])

    total = take(z).astype(F32)
    for step in (1, 7, 2, 6, 3, 5, 4):
        total = total + shift_z(take(z + step), step).astype(F32)
    return total


def local(queries, keys, values, doc_ids, w_out, cotangent):
    core = lax.axis_index("c")
    zh = lax.axis_index("zh")

    def by_core(a):
        a = a.reshape(128, 2, 2, a.shape[1] // 4)
        mine = pick(a, core, 2).reshape(128, -1)
        theirs = pick(a, 1 - core, 2).reshape(128, -1)
        return mine, theirs

    w_local = gather_z(w_out.T)
    w_first = gather_axis(gather_axis(w_local[0], "y", 1), "x", 1).reshape(4608, 512)
    w_second = gather_axis(gather_axis(w_local[1], "x", 1), "y", 2).reshape(4608, 512)

    q_mine, q_theirs = by_core(queries)
    k_mine, k_theirs = by_core(keys)
    v_mine, v_theirs = by_core(values)
    received = swap_core(jnp.concatenate([q_theirs, k_theirs, v_theirs], axis=1))
    q = jnp.concatenate([q_mine, received[:, :1024]], axis=0)
    kv = jnp.concatenate(
        [jnp.concatenate([k_mine, v_mine], axis=1), received[:, 1024:]], axis=0
    )
    cot = jnp.concatenate([cotangent, swap_core(cotangent)], axis=0)
    docs = jnp.concatenate([doc_ids, swap_core(doc_ids)]) + 1
    docs_before = lax.ppermute(docs, "zh", [(0, 1)])
    kv_before = lax.ppermute(kv, "zh", [(0, 1)])

    row = jnp.arange(128, dtype=jnp.int32)
    position = jnp.concatenate([core * 128 + row, (1 - core) * 128 + row])
    near = (docs[:, None] == docs[None, :]) & (position[:, None] >= position[None, :])
    far = docs[:, None] == docs_before[None, :]
    mask = jnp.concatenate([near, far], axis=1).astype(F32)

    ko, vo = kv[:, :512], kv[:, 512:]
    kx, vx = kv_before[:, :512], kv_before[:, 512:]
    att, probs, slopes = attend(q, ko, kx, vo, vx, mask)

    cot_t = cot.T
    g_first = dot(cot_t, att[:, :512]).astype(BF16).reshape(4, 4, 288, 512)
    g_second = dot(cot_t, att[:, 512:]).astype(BF16).reshape(4, 4, 4, 72, 512)
    g_first = scatter_axis(g_first, "x", 1).reshape(4, 4, 72, 512)
    g_second = scatter_axis(g_second, "y", 2)
    g_first = scatter_axis(g_first, "y", 1)
    g_second = scatter_axis(g_second, "x", 1)
    w_grad = scatter_z(g_first, g_second).T

    grads = jnp.concatenate([dot(cot, w_first), dot(cot, w_second)], axis=1).astype(BF16)
    dq, dko, dkx, dvo, dvx = attend_back(q, ko, kx, vo, vx, att, probs, slopes, grads)

    back = lax.ppermute(jnp.concatenate([dkx, dvx], axis=1), "zh", [(1, 0)])
    dkv = (jnp.concatenate([dko, dvo], axis=1) + back.astype(F32)).astype(BF16)

    partial = dot(att[:, :512], w_first, NT) + dot(att[:, 512:], w_second, NT)
    mixed = (partial[:128] + swap_core(partial[128:].astype(BF16)).astype(F32)).astype(BF16)

    def join(mine, theirs):
        mine = mine.reshape(128, 2, 1, -1)
        theirs = theirs.reshape(128, 2, 1, -1)
        low = jnp.where(core == 0, mine, theirs)
        high = jnp.where(core == 0, theirs, mine)
        return jnp.concatenate([low, high], axis=2).reshape(128, -1)

    dq_back = swap_core(dq[128:])
    dkv_back = swap_core(dkv[128:])
    return (
        mixed,
        join(dq[:128], dq_back),
        join(dkv[:128, :512], dkv_back[:, :512]),
        join(dkv[:128, 512:], dkv_back[:, 512:]),
        w_grad,
    )


def solution(mesh):
    fine = Mesh(mesh.devices.reshape(4, 4, 4, 2, 2), ("zl", "x", "y", "zh", "c"))
    tokens = ("zl", "x", "y", "zh", "c")
    rows = P(tokens, None)
    weight = P(("zh", "c"), ("zl", "x", "y"))
    return jax.shard_map(
        local,
        mesh=fine,
        in_specs=(rows, rows, rows, P(tokens), weight, rows),
        out_specs=(rows, rows, rows, rows, weight),
        check_vma=False,
    )
```

```python
import jax
import jax.numpy as jnp
from jax import lax
from jax.experimental import pallas as pl
from jax.experimental.pallas import tpu as pltpu
from jax.sharding import Mesh, PartitionSpec as P

HD = 128
SCALE = 1.0 / 12.0
CAP = 50.0
F32 = jnp.float32
BF16 = jnp.bfloat16
NT = (((1,), (1,)), ((), ()))
TN = (((0,), (0,)), ((), ()))
ANY = pl.BlockSpec(memory_space=pl.ANY)
WHOLE = pl.BlockSpec(memory_space=pltpu.VMEM)
SCALAR = pl.BlockSpec(memory_space=pltpu.SMEM)
LIMIT = 32 << 20
FREE = pl.CostEstimate(flops=0, bytes_accessed=0, transcendentals=0)


def dot(a, b, dims=(((1,), (0,)), ((), ()))):
    return lax.dot_general(a, b, dims, preferred_element_type=F32)


def shift(a, axis, step):
    return lax.ppermute(a, axis, [(i, (i + step) % 4) for i in range(4)])


def swap(a, axis):
    return lax.ppermute(a, axis, [(0, 1), (1, 0)])


def pick(a, index, axis):
    return lax.dynamic_index_in_dim(a, index, axis, keepdims=False)


def place(buffer, block, index, axis):
    return lax.dynamic_update_index_in_dim(buffer, block, index, axis)


def tie(arrays, after):
    n = len(arrays)
    out = pl.pallas_call(
        lambda *refs: None,
        in_specs=[ANY] * (n + len(after)),
        out_specs=[ANY] * n,
        out_shape=[jax.ShapeDtypeStruct(a.shape, a.dtype) for a in arrays],
        input_output_aliases={i: i for i in range(n)},
        cost_estimate=FREE,
        name="tie",
    )(*arrays, *after)
    return list(out)


def head_block(zh, core, g):
    return (zh + (g // 2) * (1 - 2 * zh)) * 2 + core


def pack_head(refs, zh, core, g):
    q_ref, k_ref, v_ref = refs
    block = head_block(zh, core, g)
    wide = pl.ds(pl.multiple_of(block * 512 + (g % 2) * 256, 256), 256)
    narrow = pl.ds(pl.multiple_of(block * 256 + (g % 2) * 128, 128), 128)
    return q_ref[:, wide], k_ref[:, narrow], v_ref[:, narrow]


def pack_kernel(core_ref, q_ref, k_ref, v_ref, doc_ref, mine_ref, theirs_ref):
    core, zh = core_ref[0], core_ref[1]
    for out_ref, who in ((mine_ref, core), (theirs_ref, 1 - core)):
        for g in range(4):
            q, k, v = pack_head((q_ref, k_ref, v_ref), zh, who, g)
            out_ref[:, g * 512 : g * 512 + 256] = q
            out_ref[:, g * 512 + 256 : g * 512 + 384] = k
            out_ref[:, g * 512 + 384 : g * 512 + 512] = v
        out_ref[:, 2048:] = doc_ref[...]


def pack(core, q, k, v, doc):
    shape = jax.ShapeDtypeStruct((128, 2176), BF16)
    return pl.pallas_call(
        pack_kernel,
        in_specs=[SCALAR, WHOLE, WHOLE, WHOLE, WHOLE],
        out_specs=[WHOLE, WHOLE],
        out_shape=[shape, shape],
        compiler_params=pltpu.CompilerParams(vmem_limit_bytes=LIMIT),
        name="pack",
    )(core, q, k, v, doc)


def pack_keys_kernel(m_ref, r_ref, *refs):
    out_ref = refs[-1]
    for rows, ref in ((slice(0, 128), m_ref), (slice(128, 256), r_ref)):
        for g in range(4):
            out_ref[rows, g * 256 : g * 256 + 256] = ref[:, g * 512 + 256 : g * 512 + 512]
        out_ref[rows, 1024:] = ref[:, 2048:]


def pack_keys(mine, theirs, after):
    return pl.pallas_call(
        pack_keys_kernel,
        in_specs=[WHOLE, WHOLE] + [ANY] * len(after),
        out_specs=WHOLE,
        out_shape=jax.ShapeDtypeStruct((256, 1152), BF16),
        compiler_params=pltpu.CompilerParams(vmem_limit_bytes=LIMIT),
        name="pack_keys",
    )(mine, theirs, *after)


def heads(m_ref, r_ref, b_ref):
    m, r, b = m_ref[...], r_ref[...], b_ref[...]
    q = jnp.concatenate([m[:, :256], r[:, :256]], axis=0)
    k = jnp.concatenate([m[:, 256:384], r[:, 256:384], b[:, :128]], axis=0)
    v = jnp.concatenate([m[:, 384:], r[:, 384:], b[:, 128:]], axis=0)
    return q, k, v


def forward_kernel(
    core_ref, m_ref, r_ref, b_ref, dm_ref, dr_ref, db_ref, att_ref, p_ref, d_ref, mask_ref
):
    core, zh = core_ref[0], core_ref[1]

    @pl.when(pl.program_id(0) == 0)
    def _():
        docs = [dm_ref[...], dr_ref[...], db_ref[:128], db_ref[128:]]
        docs = [d.astype(F32) for d in docs]
        doc_q = jnp.concatenate([jnp.concatenate(docs[:2], axis=0)] * 4, axis=1)
        doc_k = jnp.concatenate([jnp.concatenate([d.T for d in docs], axis=1)] * 2, axis=0)
        row = lax.broadcasted_iota(jnp.int32, (256, 512), 0)
        col = lax.broadcasted_iota(jnp.int32, (256, 512), 1)
        own, other = core * 128, (1 - core) * 128 - 128
        pos_q = row + jnp.where(row < 128, own, other)
        before = jnp.where(zh == 1, -1, 1024)
        pos_k = jnp.where(col < 256, col + jnp.where(col < 128, own, other), before)
        mask_ref[...] = ((doc_q == doc_k) & (pos_q >= pos_k)).astype(F32)

    q, k, v = heads(m_ref, r_ref, b_ref)
    for r in range(2):
        cols = slice(r * HD, (r + 1) * HD)
        t = jnp.tanh(dot(q[:, cols], k, NT) * (SCALE / CAP))
        w = jnp.exp(CAP * t) * mask_ref[...]
        p = w * (1.0 / jnp.sum(w, axis=-1, keepdims=True))
        rounded = p.astype(BF16)
        p_ref[r] = rounded
        d_ref[r] = p * (1.0 - t * t)
        att_ref[:, cols] = dot(rounded, v).astype(BF16)


def backward_kernel(
    m_ref, r_ref, b_ref, att_ref, p_ref, d_ref, g_ref,
    dq_ref, dq_other_ref, dkv_ref, dkv_other_ref, back_ref,
):
    q, k, v = heads(m_ref, r_ref, b_ref)
    dk = 0.0
    dv = 0.0
    for r in range(2):
        cols = slice(r * HD, (r + 1) * HD)
        g = g_ref[:, cols]
        row = jnp.sum(g.astype(F32) * att_ref[:, cols].astype(F32), axis=-1, keepdims=True)
        ds = (d_ref[r] * (dot(g, v, NT) - row)).astype(BF16)
        dq = (dot(ds, k) * SCALE).astype(BF16)
        dq_ref[:, cols] = dq[:128]
        dq_other_ref[:, cols] = dq[128:]
        dk = dk + dot(ds, q[:, cols], TN)
        dv = dv + dot(p_ref[r], g, TN)
    dk = dk * SCALE
    dkv_ref[:, :128] = dk[:128]
    dkv_ref[:, 128:] = dv[:128]
    dkv_other_ref[:, :128] = dk[128:256]
    dkv_other_ref[:, 128:] = dv[128:256]
    back_ref[:, :128] = dk[256:].astype(BF16)
    back_ref[:, 128:] = dv[256:].astype(BF16)


def block(rows, columns, last=None):
    return pl.BlockSpec((rows, columns), lambda g: (0, g) if last is None else (0, last))


def scores():
    return pl.BlockSpec((2, 256, 512), lambda g: (g, 0, 0))


PACKS = [block(128, 512), block(128, 512), pl.BlockSpec((256, 256), lambda g: (0, (g + 2) % 4))]
DOCS = [block(128, 128, 16), block(128, 128, 16), block(256, 128, 8)]


def attend(core, packs):
    return pl.pallas_call(
        forward_kernel,
        grid=(4,),
        in_specs=[SCALAR] + PACKS + DOCS,
        out_specs=[block(256, 256), scores(), scores()],
        out_shape=[
            jax.ShapeDtypeStruct((256, 1024), BF16),
            jax.ShapeDtypeStruct((8, 256, 512), BF16),
            jax.ShapeDtypeStruct((8, 256, 512), F32),
        ],
        scratch_shapes=[pltpu.VMEM((256, 512), F32)],
        cost_estimate=FREE,
        compiler_params=pltpu.CompilerParams(vmem_limit_bytes=LIMIT),
        name="attend",
    )(core, *packs, *packs)


def attend_back(packs, att, p, d, g):
    return pl.pallas_call(
        backward_kernel,
        grid=(4,),
        in_specs=PACKS + [block(256, 256), scores(), scores(), block(256, 256)],
        out_specs=[block(128, 256)] * 4 + [block(256, 256)],
        out_shape=[
            jax.ShapeDtypeStruct((128, 1024), BF16),
            jax.ShapeDtypeStruct((128, 1024), BF16),
            jax.ShapeDtypeStruct((128, 1024), F32),
            jax.ShapeDtypeStruct((128, 1024), F32),
            jax.ShapeDtypeStruct((256, 1024), BF16),
        ],
        cost_estimate=FREE,
        compiler_params=pltpu.CompilerParams(vmem_limit_bytes=LIMIT),
        name="attend_back",
    )(*packs, att, p, d, g)


def merge_kernel(dq_ref, dkv_ref, back_ref, mixed_ref, *refs):
    out_ref = refs[-1]
    out_ref[:, :1024] = dq_ref[...]
    for g in range(4):
        two = slice(g * 256, g * 256 + 256)
        flipped = slice((g + 2) % 4 * 256, (g + 2) % 4 * 256 + 256)
        out_ref[:, 1024 + g * 256 : 1280 + g * 256] = (
            dkv_ref[:, two] + back_ref[128:, flipped].astype(F32)
        ).astype(BF16)
    out_ref[:, 2048:] = mixed_ref[128:].astype(BF16)


def merge(dq, dkv, back, mixed, after):
    return pl.pallas_call(
        merge_kernel,
        in_specs=[WHOLE] * 4 + [ANY] * len(after),
        out_specs=WHOLE,
        out_shape=jax.ShapeDtypeStruct((128, 6656), BF16),
        cost_estimate=FREE,
        compiler_params=pltpu.CompilerParams(vmem_limit_bytes=LIMIT),
        name="merge",
    )(dq, dkv, back, mixed, *after)


def unpack_kernel(core_ref, dq_ref, dkv_ref, back_ref, swap_ref, q_ref, k_ref, v_ref):
    core, zh = core_ref[0], core_ref[1]
    for mine in (True, False):
        who = core if mine else 1 - core
        for g in range(4):
            part = head_block(zh, who, g)
            wide = pl.ds(pl.multiple_of(part * 512 + (g % 2) * 256, 256), 256)
            narrow = pl.ds(pl.multiple_of(part * 256 + (g % 2) * 128, 128), 128)
            two = slice(g * 256, g * 256 + 256)
            flipped = slice((g + 2) % 4 * 256, (g + 2) % 4 * 256 + 256)
            if mine:
                q = dq_ref[:, two]
                kv = (dkv_ref[:, two] + back_ref[:128, flipped].astype(F32)).astype(BF16)
            else:
                q = swap_ref[:, two]
                kv = swap_ref[:, 1024 + g * 256 : 1280 + g * 256]
            q_ref[:, wide] = q
            k_ref[:, narrow] = kv[:, :128]
            v_ref[:, narrow] = kv[:, 128:]


def unpack(core, *args):
    return pl.pallas_call(
        unpack_kernel,
        in_specs=[SCALAR] + [WHOLE] * 4,
        out_specs=[WHOLE] * 3,
        out_shape=[
            jax.ShapeDtypeStruct((128, 2048), BF16),
            jax.ShapeDtypeStruct((128, 1024), BF16),
            jax.ShapeDtypeStruct((128, 1024), BF16),
        ],
        compiler_params=pltpu.CompilerParams(vmem_limit_bytes=LIMIT),
        name="unpack",
    )(core, *args)


STEPS = (2, 1, 3)
BACK = (3, 1, 2)


def trio(block, axis):
    return [shift(block, axis, step) for step in STEPS]


def assemble(block, received, axis, at):
    me = lax.axis_index(axis)
    shape = block.shape[:at] + (4,) + block.shape[at:]
    out = place(jnp.zeros(shape, block.dtype), block, me, at)
    for step, part in zip(STEPS, received):
        out = place(out, part, (me - step) % 4, at)
    return out


def ring(block, axis):
    behind, ahead = shift(block, axis, 1), shift(block, axis, 3)
    return [behind, ahead, shift(behind[:2], axis, 1), shift(ahead[2:], axis, 3)]


def assemble_ring(block, received, axis):
    me = lax.axis_index(axis)
    behind, ahead, low, high = received
    at = 1 if block.ndim == 3 else 2
    out = place(jnp.zeros(block.shape[:at] + (4,) + block.shape[at:], block.dtype), block, me, at)
    out = place(out, behind, (me + 3) % 4, at)
    out = place(out, ahead, (me + 1) % 4, at)
    two = jnp.expand_dims(jnp.concatenate([low, high], axis=0), at)
    return lax.dynamic_update_slice_in_dim(out, two, (me + 2) % 4, at)


def add_first(part, received, at):
    total = (part[at : at + 2].astype(F32) + received.astype(F32)).astype(BF16)
    return lax.dynamic_update_slice_in_dim(part, total, at, 0)


def across(a, step):
    pairs = [(2 * i + h, 2 * ((i + step) % 4) + 1 - h) for i in range(4) for h in range(2)]
    return lax.ppermute(a, ("zl", "zh"), pairs)


def cut(blocks, axis, at):
    me = lax.axis_index(axis)
    return [pick(blocks, (me + step) % 4, at) for step in (0,) + BACK]


def send(parts, axis):
    return [shift(part, axis, step) for part, step in zip(parts, BACK)]


def add(own, received):
    total = own.astype(F32)
    for part in received:
        total = total + part.astype(F32)
    return total


def local(queries, keys, values, doc_ids, w_out, cotangent):
    core = lax.axis_index("c").astype(jnp.int32)
    zh = lax.axis_index("zh").astype(jnp.int32)
    zl = lax.axis_index("zl").astype(jnp.int32)
    who = jnp.stack([core, zh])
    doc = jnp.broadcast_to(doc_ids.astype(BF16)[:, None], (128, 128))

    own = w_out.T
    near1 = trio(own, "zl")
    far1 = [across(own, step) for step in (2, 1, 3, 0)]
    mine, theirs = pack(who, queries, keys, values, doc)
    theirs = swap(theirs, "c")
    cot_other = swap(cotangent, "c")
    near = assemble(own, near1, "zl", 0)
    far = assemble(far1[3], far1[:3], "zl", 0)
    keys_sent = pack_keys(mine, theirs, [])
    near, far = tie([near, far], [keys_sent])
    before = lax.ppermute(keys_sent, "zh", [(0, 1)])
    near2, far2 = trio(near, "y"), trio(far, "x")
    near = assemble(near, near2, "y", 1).reshape(4, 288, 512)
    far = assemble(far, far2, "x", 1)
    (near,) = tie([near], [before, cot_other])
    near3, far3 = ring(near, "x"), ring(far, "y")

    packs = [mine, theirs, before]
    att, probs, slopes = attend(who, packs)

    cot = jnp.concatenate([cotangent, cot_other], axis=0)
    cot_t = cot.T
    cot_y = cot_t.reshape(4, 4, 4, 72, 256).transpose(0, 2, 1, 3, 4).reshape(4608, 256)
    g_near = dot(cot_y, att[:, :512]).astype(BF16).reshape(4, 4, 288, 512)
    g_far = dot(cot_t, att[:, 512:]).astype(BF16).reshape(4, 4, 288, 512)
    far_own, far_behind, far_ahead, far_two = cut(g_far, "x", 1)
    near_own, near_behind, near_ahead, near_two = cut(g_near, "y", 1)
    two = tie([far_two[:2], far_two[2:], near_two[:2], near_two[2:]], near3 + far3)
    far_sent = [shift(two[0], "x", 1), shift(two[1], "x", 3)]
    near_sent = [shift(two[2], "y", 1), shift(two[3], "y", 3)]
    w_near = assemble_ring(near, near3, "x").reshape(4608, 512)
    w_far = assemble_ring(far, far3, "y").reshape(4608, 512)
    far_ahead, far_behind = add_first(far_ahead, far_sent[0], 0), add_first(far_behind, far_sent[1], 2)
    near_ahead, near_behind = add_first(near_ahead, near_sent[0], 0), add_first(near_behind, near_sent[1], 2)
    (cot,) = tie([cot], [far_ahead, far_behind, near_ahead, near_behind])
    far_sent = [shift(far_ahead, "x", 1), shift(far_behind, "x", 3)]
    near_sent = [shift(near_ahead, "y", 1), shift(near_behind, "y", 3)]

    grads = jnp.concatenate([dot(cot, w_near), dot(cot, w_far)], axis=1).astype(BF16)
    dq, dq_other, dkv, dkv_other, back = attend_back(packs, att, probs, slopes, grads)
    (att,) = tie([att], [dq])
    partial = dot(att[:, :512], w_near, NT) + dot(att[:, 512:], w_far, NT)
    back = lax.ppermute(back, "zh", [(1, 0)])

    (far_own,) = tie([far_own], [dq, back])
    g_far = add(far_own, far_sent).astype(BF16).reshape(4, 4, 72, 512)
    g_near = add(near_own, near_sent).astype(BF16).reshape(4, 4, 72, 512)
    swapped = swap(merge(dq_other, dkv_other, back, partial, [g_far]), "c")
    mixed = (partial[:128] + swapped[:, 2048:].astype(F32)).astype(BF16)
    far_cut, near_cut = cut(g_far, "y", 1), cut(g_near, "x", 1)
    far_sent, near_sent = send(far_cut[1:], "y"), send(near_cut[1:], "x")
    g_far = add(far_cut[0], far_sent).astype(BF16)
    g_near = add(near_cut[0], near_sent).astype(BF16)
    g_far, g_near = tie([g_far, g_near], [swapped])

    query_grad, key_grad, value_grad = unpack(who, dq, dkv, back, swapped)

    near_cut = cut(g_near, "zl", 0)
    far_sent = [across(pick(g_far, (zl + step) % 4, 0), step) for step in (0, 3, 1, 2)]
    w_grad = add(near_cut[0], send(near_cut[1:], "zl") + far_sent)
    return mixed, query_grad, key_grad, value_grad, w_grad.T


def solution(mesh):
    fine = Mesh(mesh.devices.reshape(4, 4, 4, 2, 2), ("zl", "x", "y", "zh", "c"))
    tokens = ("zl", "x", "y", "zh", "c")
    rows = P(tokens, None)
    weight = P(("zh", "c"), ("zl", "x", "y"))
    return jax.shard_map(
        local,
        mesh=fine,
        in_specs=(rows, rows, rows, P(tokens), weight, rows),
        out_specs=(rows, rows, rows, rows, weight),
        check_vma=False,
    )
```

```python
import jax
import jax.numpy as jnp
from jax import lax
from jax.experimental import pallas as pl
from jax.experimental.pallas import tpu as pltpu
from jax.sharding import Mesh, PartitionSpec as P

HD = 128
SCALE = 1.0 / 12.0
CAP = 50.0
F32 = jnp.float32
BF16 = jnp.bfloat16
NT = (((1,), (1,)), ((), ()))
TN = (((0,), (0,)), ((), ()))
ANY = pl.BlockSpec(memory_space=pl.ANY)
WHOLE = pl.BlockSpec(memory_space=pltpu.VMEM)
SCALAR = pl.BlockSpec(memory_space=pltpu.SMEM)
LIMIT = 32 << 20
FREE = pl.CostEstimate(flops=0, bytes_accessed=0, transcendentals=0)


def dot(a, b, dims=(((1,), (0,)), ((), ()))):
    return lax.dot_general(a, b, dims, preferred_element_type=F32)


def shift(a, axis, step):
    return lax.ppermute(a, axis, [(i, (i + step) % 4) for i in range(4)])


def swap(a, axis):
    return lax.ppermute(a, axis, [(0, 1), (1, 0)])


def pick(a, index, axis):
    return lax.dynamic_index_in_dim(a, index, axis, keepdims=False)


def place(buffer, block, index, axis):
    return lax.dynamic_update_index_in_dim(buffer, block, index, axis)


def tie(arrays, after):
    n = len(arrays)
    out = pl.pallas_call(
        lambda *refs: None,
        in_specs=[ANY] * (n + len(after)),
        out_specs=[ANY] * n,
        out_shape=[jax.ShapeDtypeStruct(a.shape, a.dtype) for a in arrays],
        input_output_aliases={i: i for i in range(n)},
        cost_estimate=FREE,
        name="tie",
    )(*arrays, *after)
    return list(out)


def head_block(zh, core, g):
    return (zh + (g // 2) * (1 - 2 * zh)) * 2 + core


def pack_head(refs, zh, core, g):
    q_ref, k_ref, v_ref = refs
    block = head_block(zh, core, g)
    wide = pl.ds(pl.multiple_of(block * 512 + (g % 2) * 256, 256), 256)
    narrow = pl.ds(pl.multiple_of(block * 256 + (g % 2) * 128, 128), 128)
    return q_ref[:, wide], k_ref[:, narrow], v_ref[:, narrow]


def pack_kernel(core_ref, q_ref, k_ref, v_ref, doc_ref, mine_ref, theirs_ref):
    core, zh = core_ref[0], core_ref[1]
    for out_ref, who in ((mine_ref, core), (theirs_ref, 1 - core)):
        for g in range(4):
            q, k, v = pack_head((q_ref, k_ref, v_ref), zh, who, g)
            out_ref[:, g * 512 : g * 512 + 256] = q
            out_ref[:, g * 512 + 256 : g * 512 + 384] = k
            out_ref[:, g * 512 + 384 : g * 512 + 512] = v
        out_ref[:, 2048:] = doc_ref[...]


def pack(core, q, k, v, doc):
    shape = jax.ShapeDtypeStruct((128, 2176), BF16)
    return pl.pallas_call(
        pack_kernel,
        in_specs=[SCALAR, WHOLE, WHOLE, WHOLE, WHOLE],
        out_specs=[WHOLE, WHOLE],
        out_shape=[shape, shape],
        compiler_params=pltpu.CompilerParams(vmem_limit_bytes=LIMIT),
        name="pack",
    )(core, q, k, v, doc)


def pack_keys_kernel(m_ref, r_ref, *refs):
    out_ref = refs[-1]
    for rows, ref in ((slice(0, 128), m_ref), (slice(128, 256), r_ref)):
        for g in range(4):
            out_ref[rows, g * 256 : g * 256 + 256] = ref[:, g * 512 + 256 : g * 512 + 512]
        out_ref[rows, 1024:] = ref[:, 2048:]


def pack_keys(mine, theirs, after):
    return pl.pallas_call(
        pack_keys_kernel,
        in_specs=[WHOLE, WHOLE] + [ANY] * len(after),
        out_specs=WHOLE,
        out_shape=jax.ShapeDtypeStruct((256, 1152), BF16),
        compiler_params=pltpu.CompilerParams(vmem_limit_bytes=LIMIT),
        name="pack_keys",
    )(mine, theirs, *after)


def heads(m_ref, r_ref, b_ref):
    m, r, b = m_ref[...], r_ref[...], b_ref[...]
    q = jnp.concatenate([m[:, :256], r[:, :256]], axis=0)
    k = jnp.concatenate([m[:, 256:384], r[:, 256:384], b[:, :128]], axis=0)
    v = jnp.concatenate([m[:, 384:], r[:, 384:], b[:, 128:]], axis=0)
    return q, k, v


def forward_kernel(
    core_ref, m_ref, r_ref, b_ref, dm_ref, dr_ref, db_ref, att_ref, p_ref, d_ref, mask_ref
):
    core, zh = core_ref[0], core_ref[1]

    @pl.when(pl.program_id(0) == 0)
    def _():
        docs = [dm_ref[...], dr_ref[...], db_ref[:128], db_ref[128:]]
        docs = [d.astype(F32) for d in docs]
        doc_q = jnp.concatenate([jnp.concatenate(docs[:2], axis=0)] * 4, axis=1)
        doc_k = jnp.concatenate([jnp.concatenate([d.T for d in docs], axis=1)] * 2, axis=0)
        row = lax.broadcasted_iota(jnp.int32, (256, 512), 0)
        col = lax.broadcasted_iota(jnp.int32, (256, 512), 1)
        own, other = core * 128, (1 - core) * 128 - 128
        pos_q = row + jnp.where(row < 128, own, other)
        before = jnp.where(zh == 1, -1, 1024)
        pos_k = jnp.where(col < 256, col + jnp.where(col < 128, own, other), before)
        mask_ref[...] = ((doc_q == doc_k) & (pos_q >= pos_k)).astype(F32)

    q, k, v = heads(m_ref, r_ref, b_ref)
    for r in range(2):
        cols = slice(r * HD, (r + 1) * HD)
        t = jnp.tanh(dot(q[:, cols], k, NT) * (SCALE / CAP))
        w = jnp.exp(CAP * t) * mask_ref[...]
        p = w * (1.0 / jnp.sum(w, axis=-1, keepdims=True))
        rounded = p.astype(BF16)
        p_ref[r] = rounded
        d_ref[r] = p * (1.0 - t * t)
        att_ref[:, cols] = dot(rounded, v).astype(BF16)


def backward_kernel(
    m_ref, r_ref, b_ref, att_ref, p_ref, d_ref, g_ref,
    dq_ref, dq_other_ref, dkv_ref, dkv_other_ref, back_ref,
):
    q, k, v = heads(m_ref, r_ref, b_ref)
    dk = 0.0
    dv = 0.0
    for r in range(2):
        cols = slice(r * HD, (r + 1) * HD)
        g = g_ref[:, cols]
        row = jnp.sum(g.astype(F32) * att_ref[:, cols].astype(F32), axis=-1, keepdims=True)
        ds = (d_ref[r] * (dot(g, v, NT) - row)).astype(BF16)
        dq = (dot(ds, k) * SCALE).astype(BF16)
        dq_ref[:, cols] = dq[:128]
        dq_other_ref[:, cols] = dq[128:]
        dk = dk + dot(ds, q[:, cols], TN)
        dv = dv + dot(p_ref[r], g, TN)
    dk = dk * SCALE
    dkv_ref[:, :128] = dk[:128]
    dkv_ref[:, 128:] = dv[:128]
    dkv_other_ref[:, :128] = dk[128:256]
    dkv_other_ref[:, 128:] = dv[128:256]
    back_ref[:, :128] = dk[256:].astype(BF16)
    back_ref[:, 128:] = dv[256:].astype(BF16)


def block(rows, columns, last=None):
    return pl.BlockSpec((rows, columns), lambda g: (0, g) if last is None else (0, last))


def scores():
    return pl.BlockSpec((2, 256, 512), lambda g: (g, 0, 0))


PACKS = [block(128, 512), block(128, 512), pl.BlockSpec((256, 256), lambda g: (0, (g + 2) % 4))]
DOCS = [block(128, 128, 16), block(128, 128, 16), block(256, 128, 8)]


def attend(core, packs):
    return pl.pallas_call(
        forward_kernel,
        grid=(4,),
        in_specs=[SCALAR] + PACKS + DOCS,
        out_specs=[block(256, 256), scores(), scores()],
        out_shape=[
            jax.ShapeDtypeStruct((256, 1024), BF16),
            jax.ShapeDtypeStruct((8, 256, 512), BF16),
            jax.ShapeDtypeStruct((8, 256, 512), F32),
        ],
        scratch_shapes=[pltpu.VMEM((256, 512), F32)],
        cost_estimate=FREE,
        compiler_params=pltpu.CompilerParams(vmem_limit_bytes=LIMIT),
        name="attend",
    )(core, *packs, *packs)


def attend_back(packs, att, p, d, g):
    return pl.pallas_call(
        backward_kernel,
        grid=(4,),
        in_specs=PACKS + [block(256, 256), scores(), scores(), block(256, 256)],
        out_specs=[block(128, 256)] * 4 + [block(256, 256)],
        out_shape=[
            jax.ShapeDtypeStruct((128, 1024), BF16),
            jax.ShapeDtypeStruct((128, 1024), BF16),
            jax.ShapeDtypeStruct((128, 1024), F32),
            jax.ShapeDtypeStruct((128, 1024), F32),
            jax.ShapeDtypeStruct((256, 1024), BF16),
        ],
        cost_estimate=FREE,
        compiler_params=pltpu.CompilerParams(vmem_limit_bytes=LIMIT),
        name="attend_back",
    )(*packs, att, p, d, g)


def merge_kernel(dq_ref, dkv_ref, back_ref, mixed_ref, *refs):
    out_ref = refs[-1]
    out_ref[:, :1024] = dq_ref[...]
    for g in range(4):
        two = slice(g * 256, g * 256 + 256)
        flipped = slice((g + 2) % 4 * 256, (g + 2) % 4 * 256 + 256)
        out_ref[:, 1024 + g * 256 : 1280 + g * 256] = (
            dkv_ref[:, two] + back_ref[128:, flipped].astype(F32)
        ).astype(BF16)
    out_ref[:, 2048:] = mixed_ref[128:].astype(BF16)


def merge(dq, dkv, back, mixed, after):
    return pl.pallas_call(
        merge_kernel,
        in_specs=[WHOLE] * 4 + [ANY] * len(after),
        out_specs=WHOLE,
        out_shape=jax.ShapeDtypeStruct((128, 6656), BF16),
        cost_estimate=FREE,
        compiler_params=pltpu.CompilerParams(vmem_limit_bytes=LIMIT),
        name="merge",
    )(dq, dkv, back, mixed, *after)


def unpack_kernel(core_ref, dq_ref, dkv_ref, back_ref, swap_ref, q_ref, k_ref, v_ref):
    core, zh = core_ref[0], core_ref[1]
    for mine in (True, False):
        who = core if mine else 1 - core
        for g in range(4):
            part = head_block(zh, who, g)
            wide = pl.ds(pl.multiple_of(part * 512 + (g % 2) * 256, 256), 256)
            narrow = pl.ds(pl.multiple_of(part * 256 + (g % 2) * 128, 128), 128)
            two = slice(g * 256, g * 256 + 256)
            flipped = slice((g + 2) % 4 * 256, (g + 2) % 4 * 256 + 256)
            if mine:
                q = dq_ref[:, two]
                kv = (dkv_ref[:, two] + back_ref[:128, flipped].astype(F32)).astype(BF16)
            else:
                q = swap_ref[:, two]
                kv = swap_ref[:, 1024 + g * 256 : 1280 + g * 256]
            q_ref[:, wide] = q
            k_ref[:, narrow] = kv[:, :128]
            v_ref[:, narrow] = kv[:, 128:]


def unpack(core, *args):
    return pl.pallas_call(
        unpack_kernel,
        in_specs=[SCALAR] + [WHOLE] * 4,
        out_specs=[WHOLE] * 3,
        out_shape=[
            jax.ShapeDtypeStruct((128, 2048), BF16),
            jax.ShapeDtypeStruct((128, 1024), BF16),
            jax.ShapeDtypeStruct((128, 1024), BF16),
        ],
        compiler_params=pltpu.CompilerParams(vmem_limit_bytes=LIMIT),
        name="unpack",
    )(core, *args)


STEPS = (2, 1, 3)
BACK = (3, 1, 2)


def trio(block, axis):
    return [shift(block, axis, step) for step in STEPS]


def assemble(block, received, axis, at):
    me = lax.axis_index(axis)
    shape = block.shape[:at] + (4,) + block.shape[at:]
    out = place(jnp.zeros(shape, block.dtype), block, me, at)
    for step, part in zip(STEPS, received):
        out = place(out, part, (me - step) % 4, at)
    return out


def ring(block, axis):
    behind, ahead = shift(block, axis, 1), shift(block, axis, 3)
    return [behind, ahead, shift(behind[:2], axis, 1), shift(ahead[2:], axis, 3)]


def assemble_ring(block, received, axis):
    me = lax.axis_index(axis)
    behind, ahead, low, high = received
    at = 1 if block.ndim == 3 else 2
    out = place(jnp.zeros(block.shape[:at] + (4,) + block.shape[at:], block.dtype), block, me, at)
    out = place(out, behind, (me + 3) % 4, at)
    out = place(out, ahead, (me + 1) % 4, at)
    two = jnp.expand_dims(jnp.concatenate([low, high], axis=0), at)
    return lax.dynamic_update_slice_in_dim(out, two, (me + 2) % 4, at)


def add_first(part, received, at):
    total = (part[at : at + 2].astype(F32) + received.astype(F32)).astype(BF16)
    return lax.dynamic_update_slice_in_dim(part, total, at, 0)


def across(a, step):
    pairs = [(2 * i + h, 2 * ((i + step) % 4) + 1 - h) for i in range(4) for h in range(2)]
    return lax.ppermute(a, ("zl", "zh"), pairs)


def cut(blocks, axis, at):
    me = lax.axis_index(axis)
    return [pick(blocks, (me + step) % 4, at) for step in (0,) + BACK]


def send(parts, axis):
    return [shift(part, axis, step) for part, step in zip(parts, BACK)]


def add(own, received):
    total = own.astype(F32)
    for part in received:
        total = total + part.astype(F32)
    return total


def local(queries, keys, values, doc_ids, w_out, cotangent):
    core = lax.axis_index("c").astype(jnp.int32)
    zh = lax.axis_index("zh").astype(jnp.int32)
    zl = lax.axis_index("zl").astype(jnp.int32)
    who = jnp.stack([core, zh])
    doc = jnp.broadcast_to(doc_ids.astype(BF16)[:, None], (128, 128))

    own = w_out.T
    near1 = trio(own, "zl")
    far1 = [across(own, step) for step in (2, 1, 3, 0)]
    mine, theirs = pack(who, queries, keys, values, doc)
    theirs = swap(theirs, "c")
    cot_other = swap(cotangent, "c")
    near = assemble(own, near1, "zl", 0)
    far = assemble(far1[3], far1[:3], "zl", 0)
    keys_sent = pack_keys(mine, theirs, [])
    near, far = tie([near, far], [keys_sent])
    before = lax.ppermute(keys_sent, "zh", [(0, 1)])
    near2, far2 = trio(near, "y"), trio(far, "x")
    near = assemble(near, near2, "y", 1).reshape(4, 288, 512)
    far = assemble(far, far2, "x", 1)
    (near,) = tie([near], [before])
    near3, far3 = ring(near, "x"), ring(far, "y")

    packs = [mine, theirs, before]
    att, probs, slopes = attend(who, packs)

    cot = jnp.concatenate([cotangent, cot_other], axis=0)
    cot_t = cot.T
    cot_y = cot_t.reshape(4, 4, 4, 72, 256).transpose(0, 2, 1, 3, 4).reshape(4608, 256)
    g_near = dot(cot_y, att[:, :512]).astype(BF16).reshape(4, 4, 288, 512)
    g_far = dot(cot_t, att[:, 512:]).astype(BF16).reshape(4, 4, 288, 512)
    far_own, far_behind, far_ahead, far_two = cut(g_far, "x", 1)
    near_own, near_behind, near_ahead, near_two = cut(g_near, "y", 1)
    two = tie([far_two[:2], far_two[2:], near_two[:2], near_two[2:]], near3 + far3)
    far_sent = [shift(two[0], "x", 1), shift(two[1], "x", 3)]
    near_sent = [shift(two[2], "y", 1), shift(two[3], "y", 3)]
    w_near = assemble_ring(near, near3, "x").reshape(4608, 512)
    w_far = assemble_ring(far, far3, "y").reshape(4608, 512)
    far_ahead, far_behind = add_first(far_ahead, far_sent[0], 0), add_first(far_behind, far_sent[1], 2)
    near_ahead, near_behind = add_first(near_ahead, near_sent[0], 0), add_first(near_behind, near_sent[1], 2)
    (cot,) = tie([cot], [far_ahead, far_behind, near_ahead, near_behind])
    far_sent = [shift(far_ahead, "x", 1), shift(far_behind, "x", 3)]
    near_sent = [shift(near_ahead, "y", 1), shift(near_behind, "y", 3)]

    grads = jnp.concatenate([dot(cot, w_near), dot(cot, w_far)], axis=1).astype(BF16)
    dq, dq_other, dkv, dkv_other, back = attend_back(packs, att, probs, slopes, grads)
    (att,) = tie([att], [dq])
    partial = dot(att[:, :512], w_near, NT) + dot(att[:, 512:], w_far, NT)
    back = lax.ppermute(back, "zh", [(1, 0)])

    (far_own,) = tie([far_own], [dq])
    g_far = add(far_own, far_sent).astype(BF16).reshape(4, 4, 72, 512)
    g_near = add(near_own, near_sent).astype(BF16).reshape(4, 4, 72, 512)
    far_cut, near_cut = cut(g_far, "y", 1), cut(g_near, "x", 1)
    far_sent, near_sent = send(far_cut[1:], "y"), send(near_cut[1:], "x")
    g_far = add(far_cut[0], far_sent).astype(BF16)
    g_near = add(near_cut[0], near_sent).astype(BF16)
    g_far, g_near = tie([g_far, g_near], [back])
    swapped = swap(merge(dq_other, dkv_other, back, partial, [g_far, g_near]), "c")
    mixed = (partial[:128] + swapped[:, 2048:].astype(F32)).astype(BF16)

    query_grad, key_grad, value_grad = unpack(who, dq, dkv, back, swapped)

    near_cut = cut(g_near, "zl", 0)
    far_sent = [across(pick(g_far, (zl + step) % 4, 0), step) for step in (0, 3, 1, 2)]
    w_grad = add(near_cut[0], send(near_cut[1:], "zl") + far_sent)
    return mixed, query_grad, key_grad, value_grad, w_grad.T


def solution(mesh):
    fine = Mesh(mesh.devices.reshape(4, 4, 4, 2, 2), ("zl", "x", "y", "zh", "c"))
    tokens = ("zl", "x", "y", "zh", "c")
    rows = P(tokens, None)
    weight = P(("zh", "c"), ("zl", "x", "y"))
    return jax.shard_map(
        local,
        mesh=fine,
        in_specs=(rows, rows, rows, P(tokens), weight, rows),
        out_specs=(rows, rows, rows, rows, weight),
        check_vma=False,
    )
```

```python
import jax
import jax.numpy as jnp
from jax import lax
from jax.experimental import pallas as pl
from jax.experimental.pallas import tpu as pltpu
from jax.sharding import Mesh, PartitionSpec as P

HD = 128
SCALE = 1.0 / 12.0
CAP = 50.0
F32 = jnp.float32
BF16 = jnp.bfloat16
NT = (((1,), (1,)), ((), ()))
TN = (((0,), (0,)), ((), ()))
ANY = pl.BlockSpec(memory_space=pl.ANY)
WHOLE = pl.BlockSpec(memory_space=pltpu.VMEM)
SCALAR = pl.BlockSpec(memory_space=pltpu.SMEM)
LIMIT = 32 << 20
FREE = pl.CostEstimate(flops=0, bytes_accessed=0, transcendentals=0)


def dot(a, b, dims=(((1,), (0,)), ((), ()))):
    return lax.dot_general(a, b, dims, preferred_element_type=F32)


def shift(a, axis, step):
    return lax.ppermute(a, axis, [(i, (i + step) % 4) for i in range(4)])


def swap(a, axis):
    return lax.ppermute(a, axis, [(0, 1), (1, 0)])


def pick(a, index, axis):
    return lax.dynamic_index_in_dim(a, index, axis, keepdims=False)


def place(buffer, block, index, axis):
    return lax.dynamic_update_index_in_dim(buffer, block, index, axis)


def tie(arrays, after):
    n = len(arrays)
    out = pl.pallas_call(
        lambda *refs: None,
        in_specs=[ANY] * (n + len(after)),
        out_specs=[ANY] * n,
        out_shape=[jax.ShapeDtypeStruct(a.shape, a.dtype) for a in arrays],
        input_output_aliases={i: i for i in range(n)},
        cost_estimate=FREE,
        name="tie",
    )(*arrays, *after)
    return list(out)


def head_block(zh, core, g):
    return (zh + (g // 2) * (1 - 2 * zh)) * 2 + core


def pack_head(refs, zh, core, g):
    q_ref, k_ref, v_ref = refs
    block = head_block(zh, core, g)
    wide = pl.ds(pl.multiple_of(block * 512 + (g % 2) * 256, 256), 256)
    narrow = pl.ds(pl.multiple_of(block * 256 + (g % 2) * 128, 128), 128)
    return q_ref[:, wide], k_ref[:, narrow], v_ref[:, narrow]


def pack_kernel(core_ref, q_ref, k_ref, v_ref, doc_ref, mine_ref, theirs_ref):
    core, zh = core_ref[0], core_ref[1]
    for out_ref, who in ((mine_ref, core), (theirs_ref, 1 - core)):
        for g in range(4):
            q, k, v = pack_head((q_ref, k_ref, v_ref), zh, who, g)
            out_ref[:, g * 512 : g * 512 + 256] = q
            out_ref[:, g * 512 + 256 : g * 512 + 384] = k
            out_ref[:, g * 512 + 384 : g * 512 + 512] = v
        out_ref[:, 2048:] = doc_ref[...]


def pack(core, q, k, v, doc):
    shape = jax.ShapeDtypeStruct((128, 2176), BF16)
    return pl.pallas_call(
        pack_kernel,
        in_specs=[SCALAR, WHOLE, WHOLE, WHOLE, WHOLE],
        out_specs=[WHOLE, WHOLE],
        out_shape=[shape, shape],
        compiler_params=pltpu.CompilerParams(vmem_limit_bytes=LIMIT),
        name="pack",
    )(core, q, k, v, doc)


def pack_keys_kernel(m_ref, r_ref, *refs):
    out_ref = refs[-1]
    for rows, ref in ((slice(0, 128), m_ref), (slice(128, 256), r_ref)):
        for g in range(4):
            out_ref[rows, g * 256 : g * 256 + 256] = ref[:, g * 512 + 256 : g * 512 + 512]
        out_ref[rows, 1024:] = ref[:, 2048:]


def pack_keys(mine, theirs, after):
    return pl.pallas_call(
        pack_keys_kernel,
        in_specs=[WHOLE, WHOLE] + [ANY] * len(after),
        out_specs=WHOLE,
        out_shape=jax.ShapeDtypeStruct((256, 1152), BF16),
        compiler_params=pltpu.CompilerParams(vmem_limit_bytes=LIMIT),
        name="pack_keys",
    )(mine, theirs, *after)


def heads(m_ref, r_ref, b_ref):
    m, r, b = m_ref[...], r_ref[...], b_ref[...]
    q = jnp.concatenate([m[:, :256], r[:, :256]], axis=0)
    k = jnp.concatenate([m[:, 256:384], r[:, 256:384], b[:, :128]], axis=0)
    v = jnp.concatenate([m[:, 384:], r[:, 384:], b[:, 128:]], axis=0)
    return q, k, v


def forward_kernel(
    core_ref, m_ref, r_ref, b_ref, dm_ref, dr_ref, db_ref, att_ref, p_ref, d_ref, mask_ref
):
    core, zh = core_ref[0], core_ref[1]

    @pl.when(pl.program_id(0) == 0)
    def _():
        docs = [dm_ref[...], dr_ref[...], db_ref[:128], db_ref[128:]]
        docs = [d.astype(F32) for d in docs]
        doc_q = jnp.concatenate([jnp.concatenate(docs[:2], axis=0)] * 4, axis=1)
        doc_k = jnp.concatenate([jnp.concatenate([d.T for d in docs], axis=1)] * 2, axis=0)
        row = lax.broadcasted_iota(jnp.int32, (256, 512), 0)
        col = lax.broadcasted_iota(jnp.int32, (256, 512), 1)
        own, other = core * 128, (1 - core) * 128 - 128
        pos_q = row + jnp.where(row < 128, own, other)
        before = jnp.where(zh == 1, -1, 1024)
        pos_k = jnp.where(col < 256, col + jnp.where(col < 128, own, other), before)
        mask_ref[...] = ((doc_q == doc_k) & (pos_q >= pos_k)).astype(F32)

    q, k, v = heads(m_ref, r_ref, b_ref)
    for r in range(2):
        cols = slice(r * HD, (r + 1) * HD)
        t = jnp.tanh(dot(q[:, cols], k, NT) * (SCALE / CAP))
        w = jnp.exp(CAP * t) * mask_ref[...]
        p = w * (1.0 / jnp.sum(w, axis=-1, keepdims=True))
        rounded = p.astype(BF16)
        p_ref[r] = rounded
        d_ref[r] = p * (1.0 - t * t)
        att_ref[:, cols] = dot(rounded, v).astype(BF16)


def backward_kernel(
    m_ref, r_ref, b_ref, att_ref, p_ref, d_ref, g_ref,
    dq_ref, dq_other_ref, dkv_ref, dkv_other_ref, back_ref,
):
    q, k, v = heads(m_ref, r_ref, b_ref)
    dk = 0.0
    dv = 0.0
    for r in range(2):
        cols = slice(r * HD, (r + 1) * HD)
        g = g_ref[:, cols]
        row = jnp.sum(g.astype(F32) * att_ref[:, cols].astype(F32), axis=-1, keepdims=True)
        ds = (d_ref[r] * (dot(g, v, NT) - row)).astype(BF16)
        dq = (dot(ds, k) * SCALE).astype(BF16)
        dq_ref[:, cols] = dq[:128]
        dq_other_ref[:, cols] = dq[128:]
        dk = dk + dot(ds, q[:, cols], TN)
        dv = dv + dot(p_ref[r], g, TN)
    dk = dk * SCALE
    dkv_ref[:, :128] = dk[:128]
    dkv_ref[:, 128:] = dv[:128]
    dkv_other_ref[:, :128] = dk[128:256]
    dkv_other_ref[:, 128:] = dv[128:256]
    back_ref[:, :128] = dk[256:].astype(BF16)
    back_ref[:, 128:] = dv[256:].astype(BF16)


def block(rows, columns, last=None):
    return pl.BlockSpec((rows, columns), lambda g: (0, g) if last is None else (0, last))


def scores():
    return pl.BlockSpec((2, 256, 512), lambda g: (g, 0, 0))


PACKS = [block(128, 512), block(128, 512), pl.BlockSpec((256, 256), lambda g: (0, (g + 2) % 4))]
DOCS = [block(128, 128, 16), block(128, 128, 16), block(256, 128, 8)]


def attend(core, packs):
    return pl.pallas_call(
        forward_kernel,
        grid=(4,),
        in_specs=[SCALAR] + PACKS + DOCS,
        out_specs=[block(256, 256), scores(), scores()],
        out_shape=[
            jax.ShapeDtypeStruct((256, 1024), BF16),
            jax.ShapeDtypeStruct((8, 256, 512), BF16),
            jax.ShapeDtypeStruct((8, 256, 512), F32),
        ],
        scratch_shapes=[pltpu.VMEM((256, 512), F32)],
        cost_estimate=FREE,
        compiler_params=pltpu.CompilerParams(vmem_limit_bytes=LIMIT),
        name="attend",
    )(core, *packs, *packs)


def attend_back(packs, att, p, d, g):
    return pl.pallas_call(
        backward_kernel,
        grid=(4,),
        in_specs=PACKS + [block(256, 256), scores(), scores(), block(256, 256)],
        out_specs=[block(128, 256)] * 4 + [block(256, 256)],
        out_shape=[
            jax.ShapeDtypeStruct((128, 1024), BF16),
            jax.ShapeDtypeStruct((128, 1024), BF16),
            jax.ShapeDtypeStruct((128, 1024), F32),
            jax.ShapeDtypeStruct((128, 1024), F32),
            jax.ShapeDtypeStruct((256, 1024), BF16),
        ],
        cost_estimate=FREE,
        compiler_params=pltpu.CompilerParams(vmem_limit_bytes=LIMIT),
        name="attend_back",
    )(*packs, att, p, d, g)


def merge_kernel(dq_ref, dkv_ref, back_ref, mixed_ref, *refs):
    out_ref = refs[-1]
    out_ref[:, :1024] = dq_ref[...]
    for g in range(4):
        two = slice(g * 256, g * 256 + 256)
        flipped = slice((g + 2) % 4 * 256, (g + 2) % 4 * 256 + 256)
        out_ref[:, 1024 + g * 256 : 1280 + g * 256] = (
            dkv_ref[:, two] + back_ref[128:, flipped].astype(F32)
        ).astype(BF16)
    out_ref[:, 2048:] = mixed_ref[...]


def merge(dq, dkv, back, mixed, after):
    return pl.pallas_call(
        merge_kernel,
        in_specs=[WHOLE] * 4 + [ANY] * len(after),
        out_specs=WHOLE,
        out_shape=jax.ShapeDtypeStruct((128, 6656), BF16),
        cost_estimate=FREE,
        compiler_params=pltpu.CompilerParams(vmem_limit_bytes=LIMIT),
        name="merge",
    )(dq, dkv, back, mixed, *after)


def unpack_kernel(core_ref, dq_ref, dkv_ref, back_ref, swap_ref, q_ref, k_ref, v_ref):
    core, zh = core_ref[0], core_ref[1]
    for mine in (True, False):
        who = core if mine else 1 - core
        for g in range(4):
            part = head_block(zh, who, g)
            wide = pl.ds(pl.multiple_of(part * 512 + (g % 2) * 256, 256), 256)
            narrow = pl.ds(pl.multiple_of(part * 256 + (g % 2) * 128, 128), 128)
            two = slice(g * 256, g * 256 + 256)
            flipped = slice((g + 2) % 4 * 256, (g + 2) % 4 * 256 + 256)
            if mine:
                q = dq_ref[:, two]
                kv = (dkv_ref[:, two] + back_ref[:128, flipped].astype(F32)).astype(BF16)
            else:
                q = swap_ref[:, two]
                kv = swap_ref[:, 1024 + g * 256 : 1280 + g * 256]
            q_ref[:, wide] = q
            k_ref[:, narrow] = kv[:, :128]
            v_ref[:, narrow] = kv[:, 128:]


def unpack(core, *args):
    return pl.pallas_call(
        unpack_kernel,
        in_specs=[SCALAR] + [WHOLE] * 4,
        out_specs=[WHOLE] * 3,
        out_shape=[
            jax.ShapeDtypeStruct((128, 2048), BF16),
            jax.ShapeDtypeStruct((128, 1024), BF16),
            jax.ShapeDtypeStruct((128, 1024), BF16),
        ],
        compiler_params=pltpu.CompilerParams(vmem_limit_bytes=LIMIT),
        name="unpack",
    )(core, *args)


STEPS = (2, 1, 3)
BACK = (3, 1, 2)


def trio(block, axis):
    return [shift(block, axis, step) for step in STEPS]


def assemble(block, received, axis, at):
    me = lax.axis_index(axis)
    shape = block.shape[:at] + (4,) + block.shape[at:]
    out = place(jnp.zeros(shape, block.dtype), block, me, at)
    for step, part in zip(STEPS, received):
        out = place(out, part, (me - step) % 4, at)
    return out


def ring(block, axis):
    behind, ahead = shift(block, axis, 1), shift(block, axis, 3)
    return [behind, ahead, shift(behind[:2], axis, 1), shift(ahead[2:], axis, 3)]


def assemble_ring(block, received, axis):
    me = lax.axis_index(axis)
    behind, ahead, low, high = received
    at = 1 if block.ndim == 3 else 2
    out = place(jnp.zeros(block.shape[:at] + (4,) + block.shape[at:], block.dtype), block, me, at)
    out = place(out, behind, (me + 3) % 4, at)
    out = place(out, ahead, (me + 1) % 4, at)
    two = jnp.expand_dims(jnp.concatenate([low, high], axis=0), at)
    return lax.dynamic_update_slice_in_dim(out, two, (me + 2) % 4, at)


def add_first(part, received, at):
    total = (part[at : at + 2].astype(F32) + received.astype(F32)).astype(BF16)
    return lax.dynamic_update_slice_in_dim(part, total, at, 0)


def across(a, step):
    pairs = [(2 * i + h, 2 * ((i + step) % 4) + 1 - h) for i in range(4) for h in range(2)]
    return lax.ppermute(a, ("zl", "zh"), pairs)


def cut(blocks, axis, at):
    me = lax.axis_index(axis)
    return [pick(blocks, (me + step) % 4, at) for step in (0,) + BACK]


def send(parts, axis):
    return [shift(part, axis, step) for part, step in zip(parts, BACK)]


def add(own, received):
    total = own.astype(F32)
    for part in received:
        total = total + part.astype(F32)
    return total


def local(queries, keys, values, doc_ids, w_out, cotangent):
    core = lax.axis_index("c").astype(jnp.int32)
    zh = lax.axis_index("zh").astype(jnp.int32)
    zl = lax.axis_index("zl").astype(jnp.int32)
    who = jnp.stack([core, zh])
    doc = jnp.broadcast_to(doc_ids.astype(BF16)[:, None], (128, 128))

    own = w_out.T
    near1 = trio(own, "zl")
    far1 = [across(own, step) for step in (2, 1, 3, 0)]
    mine, theirs = pack(who, queries, keys, values, doc)
    theirs = swap(theirs, "c")
    cot_other = swap(cotangent, "c")
    near = assemble(own, near1, "zl", 0)
    far = assemble(far1[3], far1[:3], "zl", 0)
    keys_sent = pack_keys(mine, theirs, [])
    near, far = tie([near, far], [keys_sent])
    before = lax.ppermute(keys_sent, "zh", [(0, 1)])
    near2, far2 = trio(near, "y"), trio(far, "x")
    near = assemble(near, near2, "y", 1).reshape(4, 288, 512)
    far = assemble(far, far2, "x", 1)
    (near,) = tie([near], [before])
    near3, far3 = ring(near, "x"), ring(far, "y")

    packs = [mine, theirs, before]
    att, probs, slopes = attend(who, packs)

    cot = jnp.concatenate([cotangent, cot_other], axis=0)
    cot_t = cot.T
    cot_y = cot_t.reshape(4, 4, 4, 72, 256).transpose(0, 2, 1, 3, 4).reshape(4608, 256)
    g_near = dot(cot_y, att[:, :512]).astype(BF16).reshape(4, 4, 288, 512)
    g_far = dot(cot_t, att[:, 512:]).astype(BF16).reshape(4, 4, 288, 512)
    far_own, far_behind, far_ahead, far_two = cut(g_far, "x", 1)
    near_own, near_behind, near_ahead, near_two = cut(g_near, "y", 1)
    two = tie([far_two[:2], far_two[2:], near_two[:2], near_two[2:]], near3 + far3)
    far_sent = [shift(two[0], "x", 1), shift(two[1], "x", 3)]
    near_sent = [shift(two[2], "y", 1), shift(two[3], "y", 3)]
    w_near = assemble_ring(near, near3, "x").reshape(4608, 512)
    w_far = assemble_ring(far, far3, "y").reshape(4608, 512)
    far_ahead, far_behind = add_first(far_ahead, far_sent[0], 0), add_first(far_behind, far_sent[1], 2)
    near_ahead, near_behind = add_first(near_ahead, near_sent[0], 0), add_first(near_behind, near_sent[1], 2)
    (cot,) = tie([cot], [far_ahead, far_behind, near_ahead, near_behind])
    far_sent = [shift(far_ahead, "x", 1), shift(far_behind, "x", 3)]
    near_sent = [shift(near_ahead, "y", 1), shift(near_behind, "y", 3)]

    grads = jnp.concatenate([dot(cot, w_near), dot(cot, w_far)], axis=1).astype(BF16)
    dq, dq_other, dkv, dkv_other, back = attend_back(packs, att, probs, slopes, grads)
    (att,) = tie([att], [dq])
    partial = dot(att[:, :512], w_near, NT) + dot(att[:, 512:], w_far, NT)
    back = lax.ppermute(back, "zh", [(1, 0)])

    (far_own,) = tie([far_own], [dq])
    g_far = add(far_own, far_sent).astype(BF16).reshape(4, 4, 72, 512)
    g_near = add(near_own, near_sent).astype(BF16).reshape(4, 4, 72, 512)
    far_cut, near_cut = cut(g_far, "y", 1), cut(g_near, "x", 1)
    far_sent, near_sent = send(far_cut[1:], "y"), send(near_cut[1:], "x")
    g_far = add(far_cut[0], far_sent).astype(BF16)
    g_near = add(near_cut[0], near_sent).astype(BF16)
    g_far, g_near = tie([g_far, g_near], [back])
    swapped = swap(merge(dq_other, dkv_other, back, partial[128:].astype(BF16), [g_far, g_near]), "c")
    mixed = (partial[:128] + swapped[:, 2048:].astype(F32)).astype(BF16)

    query_grad, key_grad, value_grad = unpack(who, dq, dkv, back, swapped)

    near_cut = cut(g_near, "zl", 0)
    far_sent = [across(pick(g_far, (zl + step) % 4, 0), step) for step in (0, 3, 1, 2)]
    w_grad = add(near_cut[0], send(near_cut[1:], "zl") + far_sent)
    return mixed, query_grad, key_grad, value_grad, w_grad.T


def solution(mesh):
    fine = Mesh(mesh.devices.reshape(4, 4, 4, 2, 2), ("zl", "x", "y", "zh", "c"))
    tokens = ("zl", "x", "y", "zh", "c")
    rows = P(tokens, None)
    weight = P(("zh", "c"), ("zl", "x", "y"))
    return jax.shard_map(
        local,
        mesh=fine,
        in_specs=(rows, rows, rows, P(tokens), weight, rows),
        out_specs=(rows, rows, rows, rows, weight),
        check_vma=False,
    )
```

```python
import jax
import jax.numpy as jnp
from jax import lax
from jax.experimental import pallas as pl
from jax.experimental.pallas import tpu as pltpu
from jax.sharding import Mesh, PartitionSpec as P

HD = 128
SCALE = 1.0 / 12.0
CAP = 50.0
F32 = jnp.float32
BF16 = jnp.bfloat16
NT = (((1,), (1,)), ((), ()))
TN = (((0,), (0,)), ((), ()))
ANY = pl.BlockSpec(memory_space=pl.ANY)
WHOLE = pl.BlockSpec(memory_space=pltpu.VMEM)
SCALAR = pl.BlockSpec(memory_space=pltpu.SMEM)
LIMIT = 32 << 20
FREE = pl.CostEstimate(flops=0, bytes_accessed=0, transcendentals=0)


def dot(a, b, dims=(((1,), (0,)), ((), ()))):
    return lax.dot_general(a, b, dims, preferred_element_type=F32)


def shift(a, axis, step):
    return lax.ppermute(a, axis, [(i, (i + step) % 4) for i in range(4)])


def swap(a, axis):
    return lax.ppermute(a, axis, [(0, 1), (1, 0)])


def pick(a, index, axis):
    return lax.dynamic_index_in_dim(a, index, axis, keepdims=False)


def place(buffer, block, index, axis):
    return lax.dynamic_update_index_in_dim(buffer, block, index, axis)


def tie(arrays, after):
    n = len(arrays)
    out = pl.pallas_call(
        lambda *refs: None,
        in_specs=[ANY] * (n + len(after)),
        out_specs=[ANY] * n,
        out_shape=[jax.ShapeDtypeStruct(a.shape, a.dtype) for a in arrays],
        input_output_aliases={i: i for i in range(n)},
        cost_estimate=FREE,
        name="tie",
    )(*arrays, *after)
    return list(out)


def head_block(zh, core, g):
    return (zh + (g // 2) * (1 - 2 * zh)) * 2 + core


def pack_head(refs, zh, core, g):
    q_ref, k_ref, v_ref = refs
    block = head_block(zh, core, g)
    wide = pl.ds(pl.multiple_of(block * 512 + (g % 2) * 256, 256), 256)
    narrow = pl.ds(pl.multiple_of(block * 256 + (g % 2) * 128, 128), 128)
    return q_ref[:, wide], k_ref[:, narrow], v_ref[:, narrow]


def pack_kernel(core_ref, q_ref, k_ref, v_ref, doc_ref, mine_ref, theirs_ref):
    core, zh = core_ref[0], core_ref[1]
    for out_ref, who in ((mine_ref, core), (theirs_ref, 1 - core)):
        for g in range(4):
            q, k, v = pack_head((q_ref, k_ref, v_ref), zh, who, g)
            out_ref[:, g * 512 : g * 512 + 256] = q
            out_ref[:, g * 512 + 256 : g * 512 + 384] = k
            out_ref[:, g * 512 + 384 : g * 512 + 512] = v
        out_ref[:, 2048:] = doc_ref[...]


def pack(core, q, k, v, doc):
    shape = jax.ShapeDtypeStruct((128, 2176), BF16)
    return pl.pallas_call(
        pack_kernel,
        in_specs=[SCALAR, WHOLE, WHOLE, WHOLE, WHOLE],
        out_specs=[WHOLE, WHOLE],
        out_shape=[shape, shape],
        compiler_params=pltpu.CompilerParams(vmem_limit_bytes=LIMIT),
        name="pack",
    )(core, q, k, v, doc)


def pack_keys_kernel(m_ref, r_ref, *refs):
    out_ref = refs[-1]
    for rows, ref in ((slice(0, 128), m_ref), (slice(128, 256), r_ref)):
        for g in range(4):
            out_ref[rows, g * 256 : g * 256 + 256] = ref[:, g * 512 + 256 : g * 512 + 512]
        out_ref[rows, 1024:] = ref[:, 2048:]


def pack_keys(mine, theirs, after):
    return pl.pallas_call(
        pack_keys_kernel,
        in_specs=[WHOLE, WHOLE] + [ANY] * len(after),
        out_specs=WHOLE,
        out_shape=jax.ShapeDtypeStruct((256, 1152), BF16),
        compiler_params=pltpu.CompilerParams(vmem_limit_bytes=LIMIT),
        name="pack_keys",
    )(mine, theirs, *after)


def heads(m_ref, r_ref, b_ref):
    m, r, b = m_ref[...], r_ref[...], b_ref[...]
    q = jnp.concatenate([m[:, :256], r[:, :256]], axis=0)
    k = jnp.concatenate([m[:, 256:384], r[:, 256:384], b[:, :128]], axis=0)
    v = jnp.concatenate([m[:, 384:], r[:, 384:], b[:, 128:]], axis=0)
    return q, k, v


def forward_kernel(
    core_ref, m_ref, r_ref, b_ref, dm_ref, dr_ref, db_ref, att_ref, p_ref, d_ref, mask_ref
):
    core, zh = core_ref[0], core_ref[1]

    @pl.when(pl.program_id(0) == 0)
    def _():
        docs = [dm_ref[...], dr_ref[...], db_ref[:128], db_ref[128:]]
        docs = [d.astype(F32) for d in docs]
        doc_q = jnp.concatenate([jnp.concatenate(docs[:2], axis=0)] * 4, axis=1)
        doc_k = jnp.concatenate([jnp.concatenate([d.T for d in docs], axis=1)] * 2, axis=0)
        row = lax.broadcasted_iota(jnp.int32, (256, 512), 0)
        col = lax.broadcasted_iota(jnp.int32, (256, 512), 1)
        own, other = core * 128, (1 - core) * 128 - 128
        pos_q = row + jnp.where(row < 128, own, other)
        before = jnp.where(zh == 1, -1, 1024)
        pos_k = jnp.where(col < 256, col + jnp.where(col < 128, own, other), before)
        mask_ref[...] = ((doc_q == doc_k) & (pos_q >= pos_k)).astype(F32)

    q, k, v = heads(m_ref, r_ref, b_ref)
    for r in range(2):
        cols = slice(r * HD, (r + 1) * HD)
        t = jnp.tanh(dot(q[:, cols], k, NT) * (SCALE / CAP))
        w = jnp.exp(CAP * t) * mask_ref[...]
        p = w * (1.0 / jnp.sum(w, axis=-1, keepdims=True))
        rounded = p.astype(BF16)
        p_ref[r] = rounded
        d_ref[r] = p * (1.0 - t * t)
        att_ref[:, cols] = dot(rounded, v).astype(BF16)


def backward_kernel(
    m_ref, r_ref, b_ref, att_ref, p_ref, d_ref, g_ref,
    dq_ref, dq_other_ref, dkv_ref, dkv_other_ref, back_ref,
):
    q, k, v = heads(m_ref, r_ref, b_ref)
    dk = 0.0
    dv = 0.0
    for r in range(2):
        cols = slice(r * HD, (r + 1) * HD)
        g = g_ref[:, cols]
        row = jnp.sum(g.astype(F32) * att_ref[:, cols].astype(F32), axis=-1, keepdims=True)
        ds = (d_ref[r] * (dot(g, v, NT) - row)).astype(BF16)
        dq = (dot(ds, k) * SCALE).astype(BF16)
        dq_ref[:, cols] = dq[:128]
        dq_other_ref[:, cols] = dq[128:]
        dk = dk + dot(ds, q[:, cols], TN)
        dv = dv + dot(p_ref[r], g, TN)
    dk = dk * SCALE
    dkv_ref[:, :128] = dk[:128]
    dkv_ref[:, 128:] = dv[:128]
    dkv_other_ref[:, :128] = dk[128:256]
    dkv_other_ref[:, 128:] = dv[128:256]
    back_ref[:, :128] = dk[256:].astype(BF16)
    back_ref[:, 128:] = dv[256:].astype(BF16)


def block(rows, columns, last=None):
    return pl.BlockSpec((rows, columns), lambda g: (0, g) if last is None else (0, last))


def scores():
    return pl.BlockSpec((2, 256, 512), lambda g: (g, 0, 0))


PACKS = [block(128, 512), block(128, 512), pl.BlockSpec((256, 256), lambda g: (0, (g + 2) % 4))]
DOCS = [block(128, 128, 16), block(128, 128, 16), block(256, 128, 8)]


def attend(core, packs):
    return pl.pallas_call(
        forward_kernel,
        grid=(4,),
        in_specs=[SCALAR] + PACKS + DOCS,
        out_specs=[block(256, 256), scores(), scores()],
        out_shape=[
            jax.ShapeDtypeStruct((256, 1024), BF16),
            jax.ShapeDtypeStruct((8, 256, 512), BF16),
            jax.ShapeDtypeStruct((8, 256, 512), F32),
        ],
        scratch_shapes=[pltpu.VMEM((256, 512), F32)],
        cost_estimate=FREE,
        compiler_params=pltpu.CompilerParams(vmem_limit_bytes=LIMIT),
        name="attend",
    )(core, *packs, *packs)


def attend_back(packs, att, p, d, g):
    return pl.pallas_call(
        backward_kernel,
        grid=(4,),
        in_specs=PACKS + [block(256, 256), scores(), scores(), block(256, 256)],
        out_specs=[block(128, 256)] * 4 + [block(256, 256)],
        out_shape=[
            jax.ShapeDtypeStruct((128, 1024), BF16),
            jax.ShapeDtypeStruct((128, 1024), BF16),
            jax.ShapeDtypeStruct((128, 1024), F32),
            jax.ShapeDtypeStruct((128, 1024), F32),
            jax.ShapeDtypeStruct((256, 1024), BF16),
        ],
        cost_estimate=FREE,
        compiler_params=pltpu.CompilerParams(vmem_limit_bytes=LIMIT),
        name="attend_back",
    )(*packs, att, p, d, g)


def merge_kernel(dq_ref, dkv_ref, back_ref, mixed_ref, *refs):
    out_ref = refs[-1]
    out_ref[:, :1024] = dq_ref[...]
    for g in range(4):
        two = slice(g * 256, g * 256 + 256)
        flipped = slice((g + 2) % 4 * 256, (g + 2) % 4 * 256 + 256)
        out_ref[:, 1024 + g * 256 : 1280 + g * 256] = (
            dkv_ref[:, two] + back_ref[128:, flipped].astype(F32)
        ).astype(BF16)
    out_ref[:, 2048:] = mixed_ref[...]


def merge(dq, dkv, back, mixed, after):
    return pl.pallas_call(
        merge_kernel,
        in_specs=[WHOLE] * 4 + [ANY] * len(after),
        out_specs=WHOLE,
        out_shape=jax.ShapeDtypeStruct((128, 6656), BF16),
        cost_estimate=FREE,
        compiler_params=pltpu.CompilerParams(vmem_limit_bytes=LIMIT),
        name="merge",
    )(dq, dkv, back, mixed, *after)


def unpack_kernel(core_ref, dq_ref, dkv_ref, back_ref, swap_ref, q_ref, k_ref, v_ref):
    core, zh = core_ref[0], core_ref[1]
    for mine in (True, False):
        who = core if mine else 1 - core
        for g in range(4):
            part = head_block(zh, who, g)
            wide = pl.ds(pl.multiple_of(part * 512 + (g % 2) * 256, 256), 256)
            narrow = pl.ds(pl.multiple_of(part * 256 + (g % 2) * 128, 128), 128)
            two = slice(g * 256, g * 256 + 256)
            flipped = slice((g + 2) % 4 * 256, (g + 2) % 4 * 256 + 256)
            if mine:
                q = dq_ref[:, two]
                kv = (dkv_ref[:, two] + back_ref[:128, flipped].astype(F32)).astype(BF16)
            else:
                q = swap_ref[:, two]
                kv = swap_ref[:, 1024 + g * 256 : 1280 + g * 256]
            q_ref[:, wide] = q
            k_ref[:, narrow] = kv[:, :128]
            v_ref[:, narrow] = kv[:, 128:]


def unpack(core, *args):
    return pl.pallas_call(
        unpack_kernel,
        in_specs=[SCALAR] + [WHOLE] * 4,
        out_specs=[WHOLE] * 3,
        out_shape=[
            jax.ShapeDtypeStruct((128, 2048), BF16),
            jax.ShapeDtypeStruct((128, 1024), BF16),
            jax.ShapeDtypeStruct((128, 1024), BF16),
        ],
        compiler_params=pltpu.CompilerParams(vmem_limit_bytes=LIMIT),
        name="unpack",
    )(core, *args)


STEPS = (2, 1, 3)
BACK = (3, 1, 2)


def trio(block, axis):
    return [shift(block, axis, step) for step in STEPS]


def assemble(block, received, axis, at):
    me = lax.axis_index(axis)
    shape = block.shape[:at] + (4,) + block.shape[at:]
    out = place(jnp.zeros(shape, block.dtype), block, me, at)
    for step, part in zip(STEPS, received):
        out = place(out, part, (me - step) % 4, at)
    return out


def ring(block, axis):
    behind, ahead = shift(block, axis, 1), shift(block, axis, 3)
    return [behind, ahead, shift(behind[:2], axis, 1), shift(ahead[2:], axis, 3)]


def assemble_ring(block, received, axis):
    me = lax.axis_index(axis)
    behind, ahead, low, high = received
    at = 1 if block.ndim == 3 else 2
    out = place(jnp.zeros(block.shape[:at] + (4,) + block.shape[at:], block.dtype), block, me, at)
    out = place(out, behind, (me + 3) % 4, at)
    out = place(out, ahead, (me + 1) % 4, at)
    two = jnp.expand_dims(jnp.concatenate([low, high], axis=0), at)
    return lax.dynamic_update_slice_in_dim(out, two, (me + 2) % 4, at)


def add_first(part, received, at):
    total = (part[at : at + 2].astype(F32) + received.astype(F32)).astype(BF16)
    return lax.dynamic_update_slice_in_dim(part, total, at, 0)


def across(a, step):
    pairs = [(2 * i + h, 2 * ((i + step) % 4) + 1 - h) for i in range(4) for h in range(2)]
    return lax.ppermute(a, ("zl", "zh"), pairs)


def cut(blocks, axis, at):
    me = lax.axis_index(axis)
    return [pick(blocks, (me + step) % 4, at) for step in (0,) + BACK]


def send(parts, axis):
    return [shift(part, axis, step) for part, step in zip(parts, BACK)]


def add(own, received):
    total = own.astype(F32)
    for part in received:
        total = total + part.astype(F32)
    return total


def local(queries, keys, values, doc_ids, w_out, cotangent):
    core = lax.axis_index("c").astype(jnp.int32)
    zh = lax.axis_index("zh").astype(jnp.int32)
    zl = lax.axis_index("zl").astype(jnp.int32)
    who = jnp.stack([core, zh])
    doc = jnp.broadcast_to(doc_ids.astype(BF16)[:, None], (128, 128))

    own = w_out.T
    near1 = trio(own, "zl")
    far1 = [across(own, step) for step in (2, 1, 3, 0)]
    mine, theirs = pack(who, queries, keys, values, doc)
    theirs = swap(theirs, "c")
    cot_other = swap(cotangent, "c")
    near = assemble(own, near1, "zl", 0)
    far = assemble(far1[3], far1[:3], "zl", 0)
    keys_sent = pack_keys(mine, theirs, [])
    near, far = tie([near, far], [keys_sent])
    before = lax.ppermute(keys_sent, "zh", [(0, 1)])
    near2, far2 = trio(near, "y"), trio(far, "x")
    near = assemble(near, near2, "y", 1).reshape(4, 288, 512)
    far = assemble(far, far2, "x", 1)
    (near,) = tie([near], [before])
    near3, far3 = ring(near, "x"), ring(far, "y")

    packs = [mine, theirs, before]
    att, probs, slopes = attend(who, packs)

    cot = jnp.concatenate([cotangent, cot_other], axis=0)
    cot_t = cot.T
    cot_y = cot_t.reshape(4, 4, 4, 72, 256).transpose(0, 2, 1, 3, 4).reshape(4608, 256)
    g_near = dot(cot_y, att[:, :512]).astype(BF16).reshape(4, 4, 288, 512)
    g_far = dot(cot_t, att[:, 512:]).astype(BF16).reshape(4, 4, 288, 512)
    far_own, far_behind, far_ahead, far_two = cut(g_far, "x", 1)
    near_own, near_behind, near_ahead, near_two = cut(g_near, "y", 1)
    two = tie([far_two[:2], far_two[2:], near_two[:2], near_two[2:]], near3 + far3)
    far_sent = [shift(two[0], "x", 1), shift(two[1], "x", 3)]
    near_sent = [shift(two[2], "y", 1), shift(two[3], "y", 3)]
    w_near = assemble_ring(near, near3, "x").reshape(4608, 512)
    w_far = assemble_ring(far, far3, "y").reshape(4608, 512)
    far_ahead, far_behind = add_first(far_ahead, far_sent[0], 0), add_first(far_behind, far_sent[1], 2)
    near_ahead, near_behind = add_first(near_ahead, near_sent[0], 0), add_first(near_behind, near_sent[1], 2)
    (cot,) = tie([cot], [far_ahead, far_behind, near_ahead, near_behind])
    far_sent = [shift(far_ahead, "x", 1), shift(far_behind, "x", 3)]
    near_sent = [shift(near_ahead, "y", 1), shift(near_behind, "y", 3)]

    grads = jnp.concatenate([dot(cot, w_near), dot(cot, w_far)], axis=1).astype(BF16)
    dq, dq_other, dkv, dkv_other, back = attend_back(packs, att, probs, slopes, grads)
    (att,) = tie([att], [dq])
    partial = dot(att[:, :512], w_near, NT) + dot(att[:, 512:], w_far, NT)
    back = lax.ppermute(back, "zh", [(1, 0)])

    (far_own,) = tie([far_own], [dq])
    g_far = add(far_own, far_sent).astype(BF16).reshape(4, 4, 72, 512)
    g_near = add(near_own, near_sent).astype(BF16).reshape(4, 4, 72, 512)
    far_cut, near_cut = cut(g_far, "y", 1), cut(g_near, "x", 1)
    far_sent, near_sent = send(far_cut[1:], "y"), send(near_cut[1:], "x")
    g_far = add(far_cut[0], far_sent).astype(BF16)
    g_near = add(near_cut[0], near_sent).astype(BF16)
    g_far, g_near = tie([g_far, g_near], [back])

    near_cut = cut(g_near, "zl", 0)
    far_sent = [across(pick(g_far, (zl + step) % 4, 0), step) for step in (0, 3, 1, 2)]
    near_sent = send(near_cut[1:], "zl")
    w_grad = add(near_cut[0], near_sent + far_sent)

    swapped = swap(merge(dq_other, dkv_other, back, partial[128:].astype(BF16), near_sent[:1]), "c")
    mixed = (partial[:128] + swapped[:, 2048:].astype(F32)).astype(BF16)
    query_grad, key_grad, value_grad = unpack(who, dq, dkv, back, swapped)
    return mixed, query_grad, key_grad, value_grad, w_grad.T


def solution(mesh):
    fine = Mesh(mesh.devices.reshape(4, 4, 4, 2, 2), ("zl", "x", "y", "zh", "c"))
    tokens = ("zl", "x", "y", "zh", "c")
    rows = P(tokens, None)
    weight = P(("zh", "c"), ("zl", "x", "y"))
    return jax.shard_map(
        local,
        mesh=fine,
        in_specs=(rows, rows, rows, P(tokens), weight, rows),
        out_specs=(rows, rows, rows, rows, weight),
        check_vma=False,
    )
```
